32 devices in a mesh: dp: 8 (over z, x), mp: 4 (over y, core).
Axes of the slice: x: 2, y: 2, z: 4, core: 2. Of those that a mesh axis runs over, the one named last changes fastest.
Arguments:
- tokens: bfloat16 [8192, 8192], P('dp', 'mp'), may hold values from -6 to 6
- value_weight: bfloat16 [8192, 1024], P('mp'), may hold values from -0.0625 to 0.0625
- adapter_down_panels: bfloat16 [24, 64, 8192], P('dp', None, 'mp'), may hold values from -0.0625 to 0.0625
- adapter_up_panels: bfloat16 [24, 64, 1024], P('dp', None, 'mp'), may hold values from -0.75 to 0.75
- cotangent: bfloat16 [8192, 1024], P('dp', 'mp'), may hold values from -6 to 6
- block_list_entry: int32 [256], P('dp'), may hold values from 0 to 7, as said below
- device_tenant_list: int32 [64], P('dp'), may hold values from 0 to 23, as said below
- tenant_location_map: int32 [24], replicated, may hold values from 0 to 23, as said below
Outputs:
- values: bfloat16 [8192, 1024], P('dp', 'mp')
- token_gradient: bfloat16 [8192, 8192], P('dp', 'mp')
- grad_a: bfloat16 [24, 64, 8192], P('dp', None, 'mp')
- grad_b: bfloat16 [24, 64, 1024], P('dp', None, 'mp')
The draws below stay inside these ranges and needn't reach their ends.
Inputs may be any that keep to these rules, and one draw needn't show every extreme that they name: `device_tenant_list`: each entry names a tenant; no tenant stands twice in one list. Of one device's 8 entries, at most 2 name tenants whose storage location tenant_location_map[t] lies on one dp index (tenant_location_map[t] // 3), and every device's list has 2 entries on some one dp index. A permutation: tenant t's panels are row tenant_location_map[t] of adapter_down_panels and adapter_up_panels. `block_list_entry`: every entry of a device's tenant list is named by at least one of that device's row blocks.
All inputs are finite; a program needn't handle non-finite values.
Results may differ from the reference program's by a relative error of at most 0.0057.
Values may be sent and summed in bfloat16 or wider, within the bound.
No kernel may reach another device: no remote copies, remote signals or barrier semaphores. Data moves between devices by JAX's collectives and lax.ppermute only.
A program may use at most 128 MiB of HBM per device.

```python
import jax
import jax.numpy as jnp
from jax import lax

MODEL_WIDTH = 8192
VALUE_WIDTH = 1024
ADAPTER_RANK = 64
BLK = 32
MOST = 2
ADP_DEV = 3
BLOCKS_DEV = 32
ROWS = 8192
TENANT_TOTAL = 24
LIST = 8
N_DP = 8


def lists_and_owners(key):
    owner_count = TENANT_TOTAL // ADP_DEV
    spots = owner_count * MOST
    placement = jax.random.permutation(jax.random.fold_in(key, 7), TENANT_TOTAL).astype(jnp.int32)
    tenant_at = jnp.argsort(placement).astype(jnp.int32)

    def one_list(device_key):
        key_one, key_two, key_three = jax.random.split(device_key, 3)
        order = jax.random.permutation(key_one, spots).astype(jnp.int32)
        holders = order // MOST
        first = holders[0]
        score = jnp.where(holders == first, 1, 0) * spots + jnp.arange(spots, dtype=jnp.int32)
        others = holders[jnp.argsort(score)][:LIST - 2]
        chosen = jnp.concatenate([jnp.stack([first, first]), others])
        chosen = chosen[jax.random.permutation(key_two, LIST)]
        entry_ids = jnp.arange(LIST, dtype=jnp.int32)
        same_holder = (chosen[:, None] == chosen[None, :]) & (entry_ids[:, None] > entry_ids[None, :])
        earlier_count = jnp.sum(jnp.where(same_holder, 1, 0), axis=1).astype(jnp.int32)
        start_row = jax.random.randint(key_three, (owner_count,), 0, ADP_DEV).astype(jnp.int32)
        local_row = (start_row[chosen] + earlier_count) % ADP_DEV
        return tenant_at[chosen * ADP_DEV + local_row]
    device_keys = jax.random.split(jax.random.fold_in(key, 8), owner_count)
    lists = jax.vmap(one_list)(device_keys).reshape(-1).astype(jnp.int32)
    return (lists, placement)


def draw_device_tenant_list(key, part):
    return lists_and_owners(key)[0]


def draw_tenant_location_map(key, part):
    return lists_and_owners(key)[1]


def draw_block_list_entry(key, part):
    owner_count = TENANT_TOTAL // ADP_DEV
    extra_count = BLOCKS_DEV - LIST

    def one_device(device_key):
        key_one, key_two, key_three, key_four = jax.random.split(device_key, 4)
        cover = jax.random.permutation(key_one, LIST).astype(jnp.int32)
        first_pick = jax.random.randint(key_two, (extra_count,), 0, LIST).astype(jnp.int32)
        second_pick = jax.random.randint(key_three, (extra_count,), 0, LIST).astype(jnp.int32)
        extra = jnp.minimum(first_pick, second_pick)
        joined = jnp.concatenate([cover, extra])
        return joined[jax.random.permutation(key_four, BLOCKS_DEV)]
    device_keys = jax.random.split(jax.random.fold_in(key, 9), owner_count)
    return jax.vmap(one_device)(device_keys).reshape(-1).astype(jnp.int32)


def block_levels(own_key, shape, shards, low, top_value):
    gain, own = 1.0, jax.random.fold_in(own_key, 6)
    for axis_at, blocks in shards:
        draws = jnp.exp(jax.random.uniform(jax.random.fold_in(own, axis_at), (blocks,), jnp.float32, low / len(shards), top_value / len(shards)))
        gain = gain * jnp.repeat(draws, shape[axis_at] // blocks).reshape([-1 if axis == axis_at else 1 for axis in range(len(shape))])
    return gain


def noise(own_key, dims, deviation, reach, cuts=(), kind=jnp.bfloat16):
    drawn = jax.random.normal(own_key, dims, jnp.float32) * deviation
    if len(cuts) > 0:
        drawn = block_levels(own_key, dims, cuts, -0.22, 0.18) * drawn
    return jnp.clip(drawn, min=-reach, max=reach).astype(kind)


def setup_inputs(seed: int = 0) -> dict:
    seeds = jax.random.split(jax.random.key(seed), 9)
    return {
        "tokens": noise(seeds[0], (ROWS, MODEL_WIDTH), 1.0, 6.0, ((0, 8), (1, 4))),
        "value_weight": noise(seeds[1], (MODEL_WIDTH, VALUE_WIDTH), MODEL_WIDTH ** -0.5, 0.0625, ((0, 4),)),
        "adapter_down_panels": noise(seeds[2], (TENANT_TOTAL, ADAPTER_RANK, MODEL_WIDTH), MODEL_WIDTH ** -0.5, 0.0625, ((0, 8), (2, 4))),
        "adapter_up_panels": noise(seeds[3], (TENANT_TOTAL, ADAPTER_RANK, VALUE_WIDTH), ADAPTER_RANK ** -0.5, 0.75, ((0, 8), (2, 4))),
        "cotangent": noise(seeds[4], (ROWS, VALUE_WIDTH), 1.0, 6.0, ((0, 8), (1, 4))),
        "block_list_entry": draw_block_list_entry(jax.random.fold_in(seeds[8], 71), 0),
        "device_tenant_list": draw_device_tenant_list(jax.random.fold_in(seeds[8], 71), 0),
        "tenant_location_map": draw_tenant_location_map(jax.random.fold_in(seeds[8], 71), 0),
    }


def reference(tokens, value_weight, adapter_down_panels, adapter_up_panels, cotangent, block_list_entry, device_tenant_list, tenant_location_map):
    token_dev = tokens.reshape(N_DP, BLOCKS_DEV, BLK, MODEL_WIDTH)
    cot_dev = cotangent.reshape(N_DP, BLOCKS_DEV, BLK, VALUE_WIDTH)
    slot_dev = block_list_entry.reshape(N_DP, BLOCKS_DEV)
    list_dev = device_tenant_list.reshape(N_DP, LIST)
    stored_ids = jnp.arange(TENANT_TOTAL, dtype=jnp.int32)

    def one_device(carry, items):
        total_a, total_b = carry
        token_blocks, cot_blocks, slot_row, list_row = items
        tenant = jnp.take(list_row, slot_row.astype(jnp.int32)).astype(jnp.int32)
        storage_location = jnp.take(tenant_location_map, tenant).astype(jnp.int32)
        block_down_panel = jnp.take(adapter_down_panels, storage_location, axis=0).astype(jnp.float32)
        block_up_panel = jnp.take(adapter_up_panels, storage_location, axis=0).astype(jnp.float32)
        token_f = token_blocks.astype(jnp.float32)
        cot_f = cot_blocks.astype(jnp.float32)
        base_output = jnp.dot(token_blocks.reshape(-1, MODEL_WIDTH), value_weight, preferred_element_type=jnp.float32)
        down_low = jnp.einsum("bnd,brd->bnr", token_f, block_down_panel).astype(jnp.bfloat16)
        down_forward = lax.optimization_barrier(down_low).astype(jnp.float32)
        adapter_output = jnp.einsum("afq,aqy->afy", down_forward, block_up_panel).reshape(-1, VALUE_WIDTH)
        values = (base_output + adapter_output).astype(jnp.bfloat16)
        up_grad = jnp.einsum("bnc,brc->bnr", cot_f, block_up_panel).astype(jnp.bfloat16)
        up_forward = lax.optimization_barrier(up_grad).astype(jnp.float32)
        base_backward_pass = jnp.dot(cot_blocks.reshape(-1, VALUE_WIDTH), value_weight.T, preferred_element_type=jnp.float32)
        adapter_backward_pass = jnp.einsum("swq,sqj->swj", up_forward, block_down_panel).reshape(-1, MODEL_WIDTH)
        token_gradient = (base_backward_pass + adapter_backward_pass).astype(jnp.bfloat16)
        block_grad_a = jnp.einsum("bnr,bnd->brd", up_forward, token_f)
        block_grad_b = jnp.einsum("bnr,bnc->brc", down_forward, cot_f)
        picker = (stored_ids[:, None] == storage_location[None, :]).astype(jnp.float32)
        share_a = jnp.einsum("lb,brd->lrd", picker, block_grad_a, precision=lax.Precision.HIGHEST).astype(jnp.bfloat16)
        share_b = jnp.einsum("lb,brc->lrc", picker, block_grad_b, precision=lax.Precision.HIGHEST).astype(jnp.bfloat16)
        share_a = lax.optimization_barrier(share_a).astype(jnp.float32)
        share_b = lax.optimization_barrier(share_b).astype(jnp.float32)
        return (total_a + share_a, total_b + share_b), (values, token_gradient)

    start = (jnp.zeros((TENANT_TOTAL, ADAPTER_RANK, MODEL_WIDTH), jnp.float32), jnp.zeros((TENANT_TOTAL, ADAPTER_RANK, VALUE_WIDTH), jnp.float32))
    totals, outputs = lax.scan(one_device, start, (token_dev, cot_dev, slot_dev, list_dev))
    values = outputs[0].reshape(ROWS, VALUE_WIDTH)
    token_gradient = outputs[1].reshape(ROWS, MODEL_WIDTH)
    return values, token_gradient, totals[0].astype(jnp.bfloat16), totals[1].astype(jnp.bfloat16)
```

```python
import jax
import jax.numpy as jnp
from jax import lax
from jax.sharding import PartitionSpec as P

F32 = jnp.float32
BF16 = jnp.bfloat16


def ring_order(n):
    cols = 1
    while 2 * (2 * cols) ** 2 <= n:
        cols *= 2
    rows = n // cols
    if cols < 2 or rows % 2 or rows * cols != n:
        return list(range(n))
    walk = [z * cols for z in range(rows)]
    for step, z in enumerate(reversed(range(rows))):
        across = range(1, cols) if step % 2 == 0 else reversed(range(1, cols))
        walk += [z * cols + x for x in across]
    return walk


def mp_sum(part, size):
    if size & (size - 1):
        return lax.psum(part, "mp")
    bit = 1
    while bit < size:
        part = part + lax.ppermute(part, "mp", [(i, i ^ bit) for i in range(size)])
        bit *= 2
    return part


def make_shards(n_dp, n_mp):
    order = ring_order(n_dp)
    place = [order.index(e) for e in range(n_dp)]
    forward = [(order[i], order[(i + 1) % n_dp]) for i in range(n_dp)]
    backward = [(b, a) for a, b in forward]
    half_way = n_dp // 2

    def shards(
        tokens,
        value_weight,
        adapter_down_panels,
        adapter_up_panels,
        cotangent,
        block_list_entry,
        device_tenant_list,
        tenant_location_map,
    ):
        rows, width = tokens.shape
        stored, rank, _ = adapter_down_panels.shape
        out_width = adapter_up_panels.shape[2]
        blocks = block_list_entry.shape[0]
        block_rows = rows // blocks
        listed = device_tenant_list.shape[0]
        tenants = tenant_location_map.shape[0]
        half = width // 2

        me = jnp.asarray(place, jnp.int32)[lax.axis_index("dp")]
        dp_at = jnp.asarray(order, jnp.int32)

        list_location = tenant_location_map[device_tenant_list]
        block_location = list_location[block_list_entry]
        row_location = jnp.repeat(block_location, block_rows)[:, None]
        row_slot = jnp.repeat(block_list_entry, block_rows)[:, None]

        up_all = lax.all_to_all(
            jnp.broadcast_to(adapter_up_panels[None], (n_dp,) + adapter_up_panels.shape),
            "dp", split_axis=0, concat_axis=0, tiled=True,
        ).reshape(tenants, rank, out_width)
        block_up = up_all[block_location]
        cot_blocks = cotangent.reshape(blocks, block_rows, out_width)
        up_part = jnp.einsum("bnc,brc->bnr", cot_blocks, block_up, preferred_element_type=F32)
        up_grad = mp_sum(up_part.reshape(rows, rank), n_mp).astype(BF16)

        from_behind, from_ahead = [adapter_down_panels], [adapter_down_panels]
        for _ in range(1, half_way):
            from_behind.append(lax.ppermute(from_behind[-1], "dp", forward))
            from_ahead.append(lax.ppermute(from_ahead[-1], "dp", backward))
        opposite = jnp.concatenate(
            [
                lax.ppermute(from_behind[-1][:, :, :half], "dp", forward),
                lax.ppermute(from_ahead[-1][:, :, half:], "dp", backward),
            ],
            axis=2,
        )
        held = jnp.concatenate(
            from_ahead + [opposite] + from_behind[:0:-1], axis=0
        )

        base_flipped = lax.psum_scatter(
            lax.dot_general(value_weight, tokens, (((0,), (1,)), ((), ())), preferred_element_type=F32),
            "mp", scatter_dimension=0, tiled=True,
        )
        cot_all = lax.all_gather(cotangent, "mp", axis=1, tiled=True)

        def spread(low, keep, count):
            eye = jnp.tile(jnp.eye(rank, dtype=BF16), (1, count))
            wide = jnp.dot(low, eye, preferred_element_type=F32)
            group = lax.broadcasted_iota(jnp.int32, (1, count * rank), 1) // rank
            return jnp.where(group == keep, wide, 0.0).astype(BF16)

        def own_share(ahead):
            dest = dp_at[(me + ahead) % n_dp]
            mine = spread(up_grad, row_location - dest * stored, stored)
            return lax.dot_general(mine, tokens, (((0,), (0,)), ((), ())), preferred_element_type=F32)

        far = own_share(half_way)
        going_ahead = far[:, :half].astype(BF16)
        going_back = far[:, half:].astype(BF16)
        ahead_sum = lax.ppermute(going_ahead, "dp", forward)
        back_sum = lax.ppermute(going_back, "dp", backward)
        zeros = jnp.zeros((stored * rank, half), F32)
        for k in range(half_way - 1, 0, -1):
            share_ahead, share_back = own_share(k), own_share(-k)
            if k == half_way - 1:
                got_ahead = jnp.concatenate([ahead_sum.astype(F32), zeros], axis=1)
                got_back = jnp.concatenate([zeros, back_sum.astype(F32)], axis=1)
            else:
                got_ahead, got_back = ahead_sum.astype(F32), back_sum.astype(F32)
            ahead_sum = lax.ppermute((share_ahead + got_ahead).astype(BF16), "dp", forward)
            back_sum = lax.ppermute((share_back + got_back).astype(BF16), "dp", backward)
        grad_a = (own_share(0) + ahead_sum.astype(F32) + back_sum.astype(F32)).astype(BF16)
        grad_a = grad_a.reshape(stored, rank, width)

        owner = list_location // stored
        ring_at = jnp.asarray(place, jnp.int32)[owner]
        held_row = ((ring_at - me) % n_dp) * stored + list_location % stored
        slot_down = held[held_row].reshape(listed * rank, width)

        down_wide = lax.dot_general(tokens, slot_down, (((1,), (1,)), ((), ())), preferred_element_type=F32)
        down_part = jnp.zeros((rows, rank), F32)
        for s in range(listed):
            down_part = down_part + jnp.where(row_slot == s, down_wide[:, s * rank:(s + 1) * rank], 0.0)
        down_low = mp_sum(down_part, n_mp).astype(BF16)
        adapter_output = jnp.einsum(
            "afq,aqy->afy", down_low.reshape(blocks, block_rows, rank), block_up, preferred_element_type=F32
        ).reshape(rows, out_width)
        values = (base_flipped.T + adapter_output).astype(BF16)

        up_wide = spread(up_grad, row_slot, listed)
        token_gradient = (
            lax.dot_general(cot_all, value_weight, (((1,), (1,)), ((), ())), preferred_element_type=F32)
            + jnp.dot(up_wide, slot_down, preferred_element_type=F32)
        ).astype(BF16)

        down_spread = spread(down_low, row_location, tenants)
        share_b = lax.dot_general(
            down_spread, cotangent, (((0,), (0,)), ((), ())), preferred_element_type=F32
        ).astype(BF16)
        back_b = lax.all_to_all(
            share_b.reshape(tenants, rank, out_width), "dp", split_axis=0, concat_axis=0, tiled=True
        ).reshape(n_dp, stored, rank, out_width)
        grad_b = jnp.sum(back_b.astype(F32), axis=0).astype(BF16)
        return (values, token_gradient, grad_a, grad_b)

    return shards


def solution(mesh):
    in_specs = (
        P("dp", "mp"),
        P("mp", None),
        P("dp", None, "mp"),
        P("dp", None, "mp"),
        P("dp", "mp"),
        P("dp"),
        P("dp"),
        P(),
    )
    out_specs = (P("dp", "mp"), P("dp", "mp"), P("dp", None, "mp"), P("dp", None, "mp"))
    shards = make_shards(mesh.shape["dp"], mesh.shape["mp"])
    return jax.shard_map(shards, mesh=mesh, in_specs=in_specs, out_specs=out_specs, check_vma=False)
```

```python
import jax
import jax.numpy as jnp
from jax import lax
from jax.experimental import pallas as pl
from jax.experimental.pallas import tpu as pltpu
from jax.sharding import PartitionSpec as P

F32 = jnp.float32
BF16 = jnp.bfloat16
MOST = 2


def grid_of(n):
    cols = 1
    while 2 * (2 * cols) ** 2 <= n:
        cols *= 2
    return (n // cols, cols) if n % cols == 0 else (n, 1)


def rows_by_need(Z):
    result = []
    for z in range(Z):
        up = {z + 1 + i: Z - 1 - i for i in range(Z - 1 - z)}
        down = {Z - z + i: i for i in range(z)}
        first, second = (up, down) if z < Z // 2 else (down, up)
        places = [None] * (Z - 1)
        for step, dest in first.items():
            places[step - 1] = dest
        rest = [dest for _, dest in sorted(second.items())]
        result.append([rest.pop(0) if p is None else p for p in places] + [z])
    return result


def lasting(us):
    return pl.CostEstimate(flops=int(us * 1.1e9), bytes_accessed=int(us * 3.4e6), transcendentals=0)


def matmul(a, b, dims=((1,), (0,))):
    return lax.dot_general(a, b, (dims, ((), ())), preferred_element_type=F32)


def after(values, others):
    count = len(values)
    return list(lax.optimization_barrier(tuple(values) + tuple(others))[:count])


def pick_panels(sources, where, which):
    slots = which.shape[0]
    _, rank, width = sources[0].shape
    n = len(sources)

    def kernel(where_ref, which_ref, *refs):
        srcs, dst, sem = refs[:n], refs[n], refs[n + 1]

        @pl.loop(0, slots)
        def _(s):
            source, panel = where_ref[s], which_ref[s]
            for b in range(n):

                @pl.when(source == b)
                def _(b=b):
                    pltpu.make_async_copy(srcs[b].at[panel], dst.at[s], sem).start()

        pltpu.make_async_copy(dst, dst, sem).wait()

    smem = pl.BlockSpec(memory_space=pltpu.SMEM)
    return pl.pallas_call(
        kernel,
        in_specs=[smem, smem] + [pl.BlockSpec(memory_space=pltpu.HBM)] * n,
        out_specs=pl.BlockSpec(memory_space=pltpu.VMEM),
        out_shape=jax.ShapeDtypeStruct((slots, rank, width), BF16),
        scratch_shapes=[pltpu.SemaphoreType.DMA],
        compiler_params=pltpu.CompilerParams(vmem_limit_bytes=32 * 1024 * 1024),
        cost_estimate=lasting(2.5),
        name="pick_panels",
    )(where, which, *sources)


def by_slot(wide, slots, rank):
    low = jnp.zeros((wide.shape[0], rank), F32)
    for s in range(wide.shape[1] // rank):
        low += jnp.where(slots == s, wide[:, s * rank:(s + 1) * rank], 0.0)
    return low


def up_products(locations, up_all, cotangent, row_slot, rank):
    rows, out_width = cotangent.shape
    listed = locations.shape[0]

    def kernel(at_ref, up_ref, cot_ref, slot_ref, part_ref, own_ref):
        for s in range(listed):
            own_ref[s * rank:(s + 1) * rank, :] = up_ref[at_ref[s]]
        low = by_slot(matmul(cot_ref[...], own_ref[...], ((1,), (1,))), slot_ref[...], rank)
        part_ref[...] = jnp.concatenate([low[:rows // 2], low[rows // 2:]], axis=1)

    vmem = pl.BlockSpec(memory_space=pltpu.VMEM)
    return pl.pallas_call(
        kernel,
        in_specs=[pl.BlockSpec(memory_space=pltpu.SMEM), vmem, vmem, vmem],
        out_specs=[vmem, vmem],
        out_shape=[
            jax.ShapeDtypeStruct((rows // 2, 2 * rank), F32),
            jax.ShapeDtypeStruct((listed * rank, out_width), BF16),
        ],
        compiler_params=pltpu.CompilerParams(vmem_limit_bytes=48 * 1024 * 1024),
        cost_estimate=lasting(2.5),
        name="up_products",
    )(locations, up_all, cotangent, row_slot)


def down_products(tokens, slot_down, row_slot, rank):
    rows, width = tokens.shape
    tile = min(256, rows // 2)
    steps = rows // 2 // tile

    def kernel(first_ref, second_ref, down_ref, slot_a_ref, slot_b_ref, part_ref):
        halves = [
            by_slot(matmul(tok[...], down_ref[...], ((1,), (1,))), slot[...], rank)
            for tok, slot in ((first_ref, slot_a_ref), (second_ref, slot_b_ref))
        ]
        part_ref[...] = jnp.concatenate(halves, axis=1)

    upper, lower = lambda i: (i, 0), lambda i: (i + steps, 0)
    return pl.pallas_call(
        kernel,
        grid=(steps,),
        in_specs=[
            pl.BlockSpec((tile, width), upper),
            pl.BlockSpec((tile, width), lower),
            pl.BlockSpec(slot_down.shape, lambda i: (0, 0)),
            pl.BlockSpec((tile, 1), upper),
            pl.BlockSpec((tile, 1), lower),
        ],
        out_specs=pl.BlockSpec((tile, 2 * rank), upper),
        out_shape=jax.ShapeDtypeStruct((rows // 2, 2 * rank), F32),
        compiler_params=pltpu.CompilerParams(vmem_limit_bytes=48 * 1024 * 1024),
        cost_estimate=lasting(4.6),
        name="down_products",
    )(tokens, tokens, slot_down, row_slot, row_slot)


def share_panels(positions, parts, row_slot, other, sizes):
    half_rows, pair = parts[0].shape
    rank, rows = pair // 2, 2 * half_rows
    listed, width = positions.shape[0], other.shape[1]
    tile = min(512, width)
    panels = sum(sizes)

    def kernel(at_ref, a_ref, b_ref, slot_ref, other_ref, wide_ref, *refs):
        out_refs, turned_ref, all_ref = refs[:-2], refs[-2], refs[-1]

        @pl.when(pl.program_id(0) == 0)
        def _():
            both = a_ref[...] + b_ref[...]
            low = jnp.concatenate([both[:, :rank], both[:, rank:]], axis=0).astype(BF16)
            column = lax.broadcasted_iota(jnp.int32, (rank, listed * rank), 1)
            eye = (column % rank == lax.broadcasted_iota(jnp.int32, (rank, listed * rank), 0)).astype(BF16)
            group = lax.broadcasted_iota(jnp.int32, (rows, listed * rank), 1) // rank
            wide = jnp.where(group == slot_ref[...], matmul(low, eye), 0.0)
            wide_ref[...] = wide.astype(BF16)
            turned_ref[...] = wide.T.astype(BF16)

        shares = matmul(turned_ref[...], other_ref[...]).astype(BF16)
        all_ref[...] = jnp.zeros(all_ref.shape, BF16)
        for s in range(listed):
            all_ref[pl.ds(pl.multiple_of(at_ref[s] * rank, rank), rank), :] = shares[s * rank:(s + 1) * rank]
        first = 0
        for ref, size in zip(out_refs, sizes):
            ref[...] = all_ref[first * rank:(first + size) * rank, :]
            first += size

    whole = lambda a: pl.BlockSpec(a.shape, lambda i, at: (0, 0))
    return pl.pallas_call(
        kernel,
        grid_spec=pltpu.PrefetchScalarGridSpec(
            num_scalar_prefetch=1,
            grid=(width // tile,),
            in_specs=[whole(parts[0]), whole(parts[1]), whole(row_slot), pl.BlockSpec((rows, tile), lambda i, at: (0, i))],
            out_specs=[pl.BlockSpec((rows, listed * rank), lambda i, at: (0, 0))]
            + [pl.BlockSpec((size * rank, tile), lambda i, at: (0, i)) for size in sizes],
            scratch_shapes=[pltpu.VMEM((listed * rank, rows), BF16), pltpu.VMEM((panels * rank, tile), BF16)],
        ),
        out_shape=[jax.ShapeDtypeStruct((rows, listed * rank), BF16)]
        + [jax.ShapeDtypeStruct((size * rank, width), BF16) for size in sizes],
        compiler_params=pltpu.CompilerParams(vmem_limit_bytes=48 * 1024 * 1024),
        cost_estimate=lasting(7.5),
        name="share_panels",
    )(positions, *parts, row_slot, other)


def add_arrivals(option, own, chosen, placing, others, stored, rank):
    width = own.shape[1]
    tile = min(512, width)
    places = [c for c, _ in chosen]
    arrays = [a for _, per_column in chosen for a in per_column]
    columns = len(placing)

    def kernel(option_ref, *refs):
        at_refs, own_refs, refs = refs[:columns], refs[columns:columns + len(places)], refs[columns + len(places):]
        got_refs, other_refs, out_ref = refs[:len(arrays)], refs[len(arrays):-1], refs[-1]

        def total_of(i):
            out = []
            for j in range(stored):
                here = slice(j * rank, (j + 1) * rank)
                total = own_refs[i][here, :].astype(F32)
                for ref in other_refs:
                    total += ref[here, :].astype(F32)
                for d in range(columns):
                    for r in range(MOST):
                        got = got_refs[i * columns + d][r * rank:(r + 1) * rank, :].astype(F32)
                        total += jnp.where(at_refs[d][places[i] * MOST + r] == j, got, 0.0)
                out_ref[here, :] = total.astype(BF16)

        if len(places) == 1:
            total_of(0)
        else:
            for i in range(len(places)):

                @pl.when(option_ref[0] == i)
                def _(i=i):
                    total_of(i)

    tall = stored * rank
    return pl.pallas_call(
        kernel,
        grid_spec=pltpu.PrefetchScalarGridSpec(
            num_scalar_prefetch=1 + columns,
            grid=(width // tile,),
            in_specs=[pl.BlockSpec((tall, tile), lambda i, *_, c=c: (c, i)) for c in places]
            + [pl.BlockSpec((MOST * rank, tile), lambda i, *_: (0, i))] * len(arrays)
            + [pl.BlockSpec((tall, tile), lambda i, *_: (0, i))] * len(others),
            out_specs=pl.BlockSpec((tall, tile), lambda i, *_: (0, i)),
        ),
        out_shape=jax.ShapeDtypeStruct((tall, width), BF16),
        compiler_params=pltpu.CompilerParams(vmem_limit_bytes=32 * 1024 * 1024),
        cost_estimate=lasting(2.5),
        name="add_arrivals",
    )(option, *[p.reshape(-1) for p in placing], *([own] * len(places)), *arrays, *others)


def base_products(mp_at, tokens, weight, count):
    rows, width = tokens.shape
    cols = weight.shape[1] // count
    tile = min(256, rows)

    def kernel(at_ref, tok_ref, *refs):
        for w, out in zip(refs[:count], refs[count:]):
            out[...] = matmul(tok_ref[...], w[...])

    return pl.pallas_call(
        kernel,
        grid_spec=pltpu.PrefetchScalarGridSpec(
            num_scalar_prefetch=1,
            grid=(rows // tile,),
            in_specs=[pl.BlockSpec((tile, width), lambda i, m: (i, 0))]
            + [pl.BlockSpec((width, cols), lambda i, m, p=p: (0, m[0] ^ p)) for p in range(count)],
            out_specs=[pl.BlockSpec((tile, cols), lambda i, m: (i, 0))] * count,
        ),
        out_shape=[jax.ShapeDtypeStruct((rows, cols), F32)] * count,
        compiler_params=pltpu.CompilerParams(vmem_limit_bytes=48 * 1024 * 1024),
        cost_estimate=lasting(8.5),
        name="base_products",
    )(mp_at, tokens, *([weight] * count))


def input_gradient(mp_at, cots, weight, up_wide, slot_down):
    rows = up_wide.shape[0]
    width = slot_down.shape[1]
    count = len(cots)
    cols = weight.shape[1] // count
    tile = min(256, rows)

    def kernel(at_ref, up_ref, slot_ref, *refs):
        total = matmul(up_ref[...], slot_ref[...])
        for c, w in zip(refs[:count], refs[count:2 * count]):
            total += matmul(c[...], w[...], ((1,), (1,)))
        refs[2 * count][...] = total.astype(BF16)

    by_row = lambda a: pl.BlockSpec((tile, a.shape[1]), lambda i, m: (i, 0))
    return pl.pallas_call(
        kernel,
        grid_spec=pltpu.PrefetchScalarGridSpec(
            num_scalar_prefetch=1,
            grid=(rows // tile,),
            in_specs=[by_row(up_wide), pl.BlockSpec(slot_down.shape, lambda i, m: (0, 0))]
            + [by_row(c) for c in cots]
            + [pl.BlockSpec((width, cols), lambda i, m, p=p: (0, m[0] ^ p)) for p in range(count)],
            out_specs=pl.BlockSpec((tile, width), lambda i, m: (i, 0)),
        ),
        out_shape=jax.ShapeDtypeStruct((rows, width), BF16),
        compiler_params=pltpu.CompilerParams(vmem_limit_bytes=48 * 1024 * 1024),
        cost_estimate=lasting(11.0),
        name="input_gradient",
    )(mp_at, up_wide, slot_down, *cots, *([weight] * count))


def make_shards(n_dp, n_mp):
    Z, X = grid_of(n_dp)
    leave = rows_by_need(Z)
    arrive = [rows[::-1] for rows in leave]

    def line(rows, step):
        return [(z * X + x, (z + step) * X + x) for z in rows for x in range(X)]

    def columns_on(d):
        return [(z * X + x, z * X + (x + d) % X) for z in range(Z) for x in range(X)]

    def source_at(z, row):
        return z - row if row <= z else Z - 1 + row - z

    needed = [sorted({source_at(z, arrive[z][k]) for z in range(Z)}) for k in range(Z)]

    def leaving_options(step, direction):
        there = range(step) if direction > 0 else range(Z - step, Z)
        return sorted({leave[z].index(z + direction * (Z - step)) for z in there})

    def leaving_option(z, step, direction):
        dest = z + direction * (Z - step)
        return leaving_options(step, direction).index(leave[z].index(dest)) if step and 0 <= dest < Z else 0

    def tables():
        result = []
        for z in range(Z):
            for x in range(X):
                result.append(
                    [z] * Z + [x] * Z + arrive[z]
                    + [needed[k].index(source_at(z, arrive[z][k])) for k in range(Z)]
                    + leave[z] + [arrive[z].index(r) for r in range(Z)] + [leave[z].index(r) for r in range(Z)]
                    + [leaving_option(z, s, 1) for s in range(Z)] + [leaving_option(z, s, -1) for s in range(Z)]
                )
        return result

    def mp_pairs(bit):
        return [(i, i ^ bit) for i in range(n_mp)]

    def shards(
        tokens,
        value_weight,
        adapter_down_panels,
        adapter_up_panels,
        cotangent,
        block_list_entry,
        device_tenant_list,
        tenant_location_map,
    ):
        rows, width = tokens.shape
        stored, rank, _ = adapter_down_panels.shape
        out_width = adapter_up_panels.shape[2]
        blocks = block_list_entry.shape[0]
        block_rows = rows // blocks
        listed = device_tenant_list.shape[0]
        tenants = tenant_location_map.shape[0]

        dp_at = lax.axis_index("dp")
        mp_at = lax.axis_index("mp")
        mp_ref = mp_at.reshape(1)
        table = lax.dynamic_index_in_dim(jnp.asarray(tables(), jnp.int32), dp_at, keepdims=False).reshape(9, Z)
        my_row, my_col, arriving, arriving_source, leaving, arrive_place, leave_place, up_option, down_option = [
            table[i] for i in range(9)
        ]
        my_row, my_col = my_row[:1], my_col[:1]

        def mp_parts(value):
            bit = 1
            while True:
                got = lax.ppermute(value, "mp", mp_pairs(bit))
                bit *= 2
                if bit >= n_mp:
                    return value, got
                value = value + got

        cots = [cotangent]
        bit = n_mp // 2
        while bit > 1:
            cots += [lax.ppermute(c, "mp", mp_pairs(bit)) for c in cots]
            bit //= 2

        up_all = lax.all_to_all(
            jnp.broadcast_to(adapter_up_panels[None], (n_dp,) + adapter_up_panels.shape),
            "dp", split_axis=0, concat_axis=0, tiled=True,
        ).reshape(tenants, rank, out_width)

        tenant_ids = jnp.arange(tenants, dtype=jnp.int32)
        list_location = jnp.sum(
            jnp.where(device_tenant_list[:, None] == tenant_ids[None, :], tenant_location_map[None, :], 0), axis=1
        )
        slot_ids = jnp.arange(listed, dtype=jnp.int32)
        row_slot = jnp.repeat(block_list_entry, block_rows)[:, None]

        def described(locations):
            holder = lax.div(locations, jnp.full_like(locations, stored))
            earlier = slot_ids[:, None] > slot_ids[None, :]
            turn = jnp.sum(jnp.where((holder[:, None] == holder[None, :]) & earlier, 1, 0), axis=1)
            cols = jnp.full_like(locations, X)
            return lax.div(holder, cols), lax.rem(holder, cols), locations - holder * stored, turn

        turns = jnp.arange(MOST, dtype=jnp.int32)

        def asked_panels(locations, places):
            row, col, panel, turn = described(locations)
            match = (
                (row[None, None, :] == places[:, None, None])
                & (col == my_col)[None, None, :]
                & (turn[None, None, :] == turns[None, :, None])
            )
            return jnp.sum(jnp.where(match, panel[None, None, :] + 1, 0), axis=2) - 1

        lists = [list_location] + [lax.ppermute(list_location, "dp", columns_on(X - d)) for d in range(1, X)]
        to_send = [None] + [jnp.maximum(asked_panels(lists[d], arriving), 0) for d in range(1, X)]
        to_place = [None] + [asked_panels(lists[X - d], leaving) for d in range(1, X)]
        row, col, panel, turn = described(list_location)
        in_row = lambda by_row: jnp.sum(
            jnp.where(row[:, None] == jnp.arange(Z, dtype=jnp.int32)[None, :], by_row[None, :], 0), axis=1
        )
        back, on = (my_col - col) & (X - 1), (col - my_col) & (X - 1)
        pick_where = jnp.where(
            back == 0,
            jnp.where(row <= my_row, my_row - row, Z - 1 + row - my_row),
            2 * Z - 1 + (back - 1) * Z + in_row(arrive_place),
        )
        pick_which = jnp.where(back == 0, panel, turn)
        leave_at = in_row(leave_place)
        share_at = jnp.where(
            on == 0, leave_at * stored + panel, Z * stored + ((on - 1) * Z + leave_at) * MOST + turn
        )

        products = base_products(mp_ref, tokens, value_weight, n_mp)
        from_core = [lax.ppermute(products[p], "mp", mp_pairs(1)) for p in range(1, n_mp, 2)]

        below, above = [adapter_down_panels], [adapter_down_panels]
        exchanged = []
        sent, placed = [], []
        up_sum = down_sum = None
        shares = None

        def leaving_sum(option, places, others):
            return add_arrivals(
                option, own_shares, [(c, placed[c]) for c in places], to_place[1:], others, stored, rank
            )

        for phase in range(2 * Z - 2):
            step, turn_out = phase + 1, phase - (Z - 2)
            if step < Z:
                below.append(lax.ppermute(below[-1], "dp", line(range(step - 1, Z - 1), 1)))
                above.append(lax.ppermute(above[-1], "dp", line(range(1, Z - step + 1), -1)))
            if phase < Z:
                sources = [below[0]] + below[1:phase + 1] + [None] * (Z - 1 - phase) + above[1:phase + 1]
                sources = [sources[i] for i in needed[phase]]
                at = jnp.broadcast_to(arriving_source[phase], (MOST,))
                exchanged.append(
                    [
                        lax.ppermute(pick_panels(sources, at, to_send[d][phase]), "dp", columns_on(d))
                        for d in range(1, X)
                    ]
                )
            if turn_out >= 0:
                placed.append([lax.ppermute(sent[d - 1][turn_out], "dp", columns_on(d)) for d in range(1, X)])
            if turn_out >= 1:
                arrived = [] if turn_out == 1 else [up_sum, down_sum]
                if turn_out <= Z // 2:
                    up_total = down_total = leaving_sum(up_option[:1], [turn_out - 1], arrived)
                else:
                    up_total = leaving_sum(
                        up_option[turn_out:turn_out + 1], leaving_options(turn_out, 1), arrived[:1]
                    )
                    down_total = leaving_sum(
                        down_option[turn_out:turn_out + 1], leaving_options(turn_out, -1), arrived[1:]
                    )
                up_sum = lax.ppermute(up_total, "dp", line(range(turn_out), 1))
                down_sum = lax.ppermute(down_total, "dp", line(range(Z - turn_out, Z), -1))

            results = ([below[-1], above[-1]] if step < Z else []) + ([up_sum, down_sum] if turn_out >= 1 else [])
            results += placed[-1] if turn_out >= 0 else []
            if phase == 0:
                results += [up_all]
            if phase == 1:
                results += from_core + cots + exchanged[0]
            if phase == 2:
                results += exchanged[1]
            results = after(results, [])
            if step < Z:
                below[-1], above[-1] = results[:2]
                results = results[2:]
            if turn_out >= 1:
                up_sum, down_sum = results[:2]
                results = results[2:]
            if turn_out >= 0:
                placed[-1], results = results[:X - 1], results[X - 1:]
            if phase == 0:
                up_part, own_ups = up_products(list_location, results[0], cotangent, row_slot, rank)
                up_parts = mp_parts(up_part)
                up_wide, own_shares, *flat_sent = share_panels(
                    share_at, up_parts, row_slot, tokens, [Z * stored] + [MOST] * (Z * (X - 1))
                )
                sent = [flat_sent[d * Z:(d + 1) * Z] for d in range(X - 1)]
            if phase == 1:
                from_core, results = results[:n_mp // 2], results[n_mp // 2:]
                cots, exchanged[0] = results[:n_mp // 2], results[n_mp // 2:]
                base = [products[p] + from_core[p // 2] for p in range(0, n_mp, 2)]
                while len(base) > 1:
                    count = len(base) // 2
                    got = [lax.ppermute(b.astype(BF16), "mp", mp_pairs(2 * count)) for b in base[count:]]
                    base = [b + g.astype(F32) for b, g in zip(base, got)]
            if phase == 2:
                exchanged[1] = results
        grad_a = leaving_sum(up_option[:1], [Z - 1], [up_sum, down_sum]).reshape(stored, rank, width)

        slot_down = pick_panels(
            below + above[1:] + [exchanged[k][d] for d in range(X - 1) for k in range(Z)], pick_where, pick_which
        ).reshape(listed * rank, width)

        down_parts = mp_parts(down_products(tokens, slot_down, row_slot, rank))
        down_wide, share_b = share_panels(list_location, down_parts, row_slot, cotangent, [tenants])
        values = (base[0] + matmul(down_wide, own_ups)).astype(BF16)

        all_cots = []
        for c in cots:
            all_cots += [c, lax.ppermute(c, "mp", mp_pairs(1))]
        token_gradient = input_gradient(mp_ref, all_cots, value_weight, up_wide, slot_down)

        back_b = lax.all_to_all(
            share_b.reshape(tenants, rank, out_width), "dp", split_axis=0, concat_axis=0, tiled=True
        ).reshape(n_dp, stored, rank, out_width)
        grad_b = jnp.sum(back_b.astype(F32), axis=0).astype(BF16)
        return (values, token_gradient, grad_a, grad_b)

    return shards


def solution(mesh):
    in_specs = (
        P("dp", "mp"),
        P("mp", None),
        P("dp", None, "mp"),
        P("dp", None, "mp"),
        P("dp", "mp"),
        P("dp"),
        P("dp"),
        P(),
    )
    out_specs = (P("dp", "mp"), P("dp", "mp"), P("dp", None, "mp"), P("dp", None, "mp"))
    shards = make_shards(mesh.shape["dp"], mesh.shape["mp"])
    return jax.shard_map(shards, mesh=mesh, in_specs=in_specs, out_specs=out_specs, check_vma=False)
```

```python
import jax
import jax.numpy as jnp
from jax import lax
from jax.experimental import pallas as pl
from jax.experimental.pallas import tpu as pltpu
from jax.sharding import PartitionSpec as P

F32 = jnp.float32
BF16 = jnp.bfloat16


def ring_order(n):
    cols = 1
    while 2 * (2 * cols) ** 2 <= n:
        cols *= 2
    rows = n // cols
    if cols < 2 or rows % 2 or rows * cols != n:
        return list(range(n))
    walk = [z * cols for z in range(rows)]
    for step, z in enumerate(reversed(range(rows))):
        across = range(1, cols) if step % 2 == 0 else reversed(range(1, cols))
        walk += [z * cols + x for x in across]
    return walk


def lasting(us):
    return pl.CostEstimate(flops=int(us * 0.05 * 1.1e9), bytes_accessed=int(us * 0.05 * 3.4e6), transcendentals=0)


def matmul(a, b, dims=((1,), (0,))):
    return lax.dot_general(a, b, (dims, ((), ())), preferred_element_type=F32)


def after(values):
    return list(lax.optimization_barrier(tuple(values)))


def pick_panels(sources, halves, where, which):
    slots = where.shape[0]
    _, rank, width = sources[0].shape
    n, cut = len(sources), width // 2

    def kernel(where_ref, which_ref, *refs):
        srcs, (left, right), dst, sem = refs[:n], refs[n:n + 2], refs[n + 2], refs[n + 3]

        @pl.loop(0, slots)
        def _(s):
            source, panel = where_ref[s], which_ref[s]
            for b in range(n):

                @pl.when(source == b)
                def _(b=b):
                    pltpu.make_async_copy(srcs[b].at[panel], dst.at[s], sem).start()

            @pl.when(source == n)
            def _():
                pltpu.make_async_copy(left.at[panel], dst.at[s, :, pl.ds(0, cut)], sem).start()
                pltpu.make_async_copy(right.at[panel], dst.at[s, :, pl.ds(cut, cut)], sem).start()

        pltpu.make_async_copy(dst, dst, sem).wait()

    smem = pl.BlockSpec(memory_space=pltpu.SMEM)
    return pl.pallas_call(
        kernel,
        in_specs=[smem, smem] + [pl.BlockSpec(memory_space=pl.ANY)] * (n + 2),
        out_specs=pl.BlockSpec(memory_space=pltpu.VMEM),
        out_shape=jax.ShapeDtypeStruct((slots, rank, width), BF16),
        scratch_shapes=[pltpu.SemaphoreType.DMA],
        compiler_params=pltpu.CompilerParams(vmem_limit_bytes=32 * 1024 * 1024),
        cost_estimate=lasting(2.5),
        name="pick_panels",
    )(where, which, *sources, *halves)


def by_slot(wide, slots, rank):
    low = jnp.zeros((wide.shape[0], rank), F32)
    for s in range(wide.shape[1] // rank):
        low += jnp.where(slots == s, wide[:, s * rank:(s + 1) * rank], 0.0)
    return low


def up_products(locations, up_all, cotangent, row_slot, rank):
    rows, out_width = cotangent.shape
    listed = locations.shape[0]

    def kernel(at_ref, up_ref, cot_ref, slot_ref, part_ref, own_ref):
        for s in range(listed):
            own_ref[s * rank:(s + 1) * rank, :] = up_ref[at_ref[s]]
        low = by_slot(matmul(cot_ref[...], own_ref[...], ((1,), (1,))), slot_ref[...], rank)
        part_ref[...] = jnp.concatenate([low[:rows // 2], low[rows // 2:]], axis=1)

    vmem = pl.BlockSpec(memory_space=pltpu.VMEM)
    return pl.pallas_call(
        kernel,
        in_specs=[pl.BlockSpec(memory_space=pltpu.SMEM), vmem, vmem, vmem],
        out_specs=[vmem, vmem],
        out_shape=[
            jax.ShapeDtypeStruct((rows // 2, 2 * rank), F32),
            jax.ShapeDtypeStruct((listed * rank, out_width), BF16),
        ],
        compiler_params=pltpu.CompilerParams(vmem_limit_bytes=48 * 1024 * 1024),
        cost_estimate=lasting(2.5),
        name="up_products",
    )(locations, up_all, cotangent, row_slot)


def down_products(tokens, slot_down, row_slot, rank):
    rows, width = tokens.shape
    tile = min(256, rows // 2)
    steps = rows // 2 // tile

    def kernel(first_ref, second_ref, down_ref, slot_a_ref, slot_b_ref, part_ref):
        halves = [
            by_slot(matmul(tok[...], down_ref[...], ((1,), (1,))), slot[...], rank)
            for tok, slot in ((first_ref, slot_a_ref), (second_ref, slot_b_ref))
        ]
        part_ref[...] = jnp.concatenate(halves, axis=1)

    upper, lower = lambda i: (i, 0), lambda i: (i + steps, 0)
    return pl.pallas_call(
        kernel,
        grid=(steps,),
        in_specs=[
            pl.BlockSpec((tile, width), upper),
            pl.BlockSpec((tile, width), lower),
            pl.BlockSpec(slot_down.shape, lambda i: (0, 0)),
            pl.BlockSpec((tile, 1), upper),
            pl.BlockSpec((tile, 1), lower),
        ],
        out_specs=pl.BlockSpec((tile, 2 * rank), upper),
        out_shape=jax.ShapeDtypeStruct((rows // 2, 2 * rank), F32),
        compiler_params=pltpu.CompilerParams(vmem_limit_bytes=48 * 1024 * 1024),
        cost_estimate=lasting(4.6),
        name="down_products",
    )(tokens, tokens, slot_down, row_slot, row_slot)


def share_panels(positions, parts, row_slot, other, panels, far=None):
    half_rows, pair = parts[0].shape
    rank, rows = pair // 2, 2 * half_rows
    listed, width = positions.shape[0], other.shape[1]
    tile = min(512, width // 2 if far else width)
    steps = width // tile

    def kernel(at_ref, a_ref, b_ref, slot_ref, other_ref, dense_ref, wide_ref, *refs):
        turned_ref = refs[-1]
        step = pl.program_id(0)

        @pl.when(step == 0)
        def _():
            both = a_ref[...] + b_ref[...]
            low = jnp.concatenate([both[:, :rank], both[:, rank:]], axis=0).astype(BF16)
            column = lax.broadcasted_iota(jnp.int32, (rank, listed * rank), 1)
            eye = (column % rank == lax.broadcasted_iota(jnp.int32, (rank, listed * rank), 0)).astype(BF16)
            group = lax.broadcasted_iota(jnp.int32, (rows, listed * rank), 1) // rank
            wide = jnp.where(group == slot_ref[...], matmul(low, eye), 0.0)
            wide_ref[...] = wide.astype(BF16)
            turned_ref[...] = wide.T.astype(BF16)

        shares = matmul(turned_ref[...], other_ref[...]).astype(BF16)
        dense_ref[...] = jnp.zeros(dense_ref.shape, BF16)
        for s in range(listed):
            dense_ref[pl.ds(pl.multiple_of(at_ref[s] * rank, rank), rank), :] = shares[s * rank:(s + 1) * rank]
        if far:
            left_ref, right_ref = refs[:2]

            @pl.when(step < steps // 2)
            def _():
                left_ref[...] = dense_ref[far[0] * rank:far[1] * rank, :]

            @pl.when(step >= steps // 2)
            def _():
                right_ref[...] = dense_ref[far[0] * rank:far[1] * rank, :]

    whole = lambda a: pl.BlockSpec(a.shape, lambda i, at: (0, 0))
    out_specs = [
        pl.BlockSpec((panels * rank, tile), lambda i, at: (0, i)),
        pl.BlockSpec((rows, listed * rank), lambda i, at: (0, 0)),
    ]
    out_shape = [
        jax.ShapeDtypeStruct((panels * rank, width), BF16),
        jax.ShapeDtypeStruct((rows, listed * rank), BF16),
    ]
    if far:
        tall = (far[1] - far[0]) * rank
        out_specs += [
            pl.BlockSpec((tall, tile), lambda i, at: (0, jnp.minimum(i, steps // 2 - 1))),
            pl.BlockSpec((tall, tile), lambda i, at: (0, jnp.maximum(i - steps // 2, 0))),
        ]
        out_shape += [jax.ShapeDtypeStruct((tall, width // 2), BF16)] * 2
    return pl.pallas_call(
        kernel,
        grid_spec=pltpu.PrefetchScalarGridSpec(
            num_scalar_prefetch=1,
            grid=(steps,),
            in_specs=[whole(parts[0]), whole(parts[1]), whole(row_slot), pl.BlockSpec((rows, tile), lambda i, at: (0, i))],
            out_specs=out_specs,
            scratch_shapes=[pltpu.VMEM((listed * rank, rows), BF16)],
        ),
        out_shape=out_shape,
        compiler_params=pltpu.CompilerParams(vmem_limit_bytes=48 * 1024 * 1024),
        cost_estimate=lasting(7.5),
        name="share_panels",
    )(positions, *parts, row_slot, other)


def add_panels(first, *others):
    rows, width = others[0].shape
    tile = min(512, width)

    def kernel(*refs):
        total = refs[0][...].astype(F32)
        for ref in refs[1:-1]:
            total += ref[...].astype(F32)
        refs[-1][...] = total.astype(BF16)

    spec = pl.BlockSpec((rows, tile), lambda i: (0, i))
    return pl.pallas_call(
        kernel,
        grid=(width // tile,),
        in_specs=[spec] * (1 + len(others)),
        out_specs=spec,
        out_shape=jax.ShapeDtypeStruct((rows, width), BF16),
        cost_estimate=lasting(260.0),
        name="add_panels",
    )(first, *others)


def base_products(mp_at, tokens, weight, count):
    rows, width = tokens.shape
    cols = weight.shape[1] // count
    tile = min(256, rows)

    def kernel(at_ref, tok_ref, *refs):
        weights, outs = refs[:count], refs[count:]
        for p in range(1, count, 2):
            outs[-1][:, p // 2 * cols:(p // 2 + 1) * cols] = matmul(tok_ref[...], weights[p][...])
        for p in range(0, count, 2):
            outs[p // 2][...] = matmul(tok_ref[...], weights[p][...])

    return pl.pallas_call(
        kernel,
        grid_spec=pltpu.PrefetchScalarGridSpec(
            num_scalar_prefetch=1,
            grid=(rows // tile,),
            in_specs=[pl.BlockSpec((tile, width), lambda i, m: (i, 0))]
            + [pl.BlockSpec((width, cols), lambda i, m, p=p: (0, m[0] ^ p)) for p in range(count)],
            out_specs=[pl.BlockSpec((tile, cols), lambda i, m: (i, 0))] * (count // 2)
            + [pl.BlockSpec((tile, count // 2 * cols), lambda i, m: (i, 0))],
        ),
        out_shape=[jax.ShapeDtypeStruct((rows, cols), F32)] * (count // 2)
        + [jax.ShapeDtypeStruct((rows, count // 2 * cols), F32)],
        compiler_params=pltpu.CompilerParams(vmem_limit_bytes=48 * 1024 * 1024),
        cost_estimate=lasting(170.0),
        name="base_products",
    )(mp_at, tokens, *([weight] * count))


def input_gradient(mp_at, cots, weight, up_wide, slot_down):
    rows = up_wide.shape[0]
    width = slot_down.shape[1]
    count = len(cots)
    cols = weight.shape[1] // count
    tile = min(256, rows)

    def kernel(at_ref, up_ref, slot_ref, *refs):
        total = matmul(up_ref[...], slot_ref[...])
        for c, w in zip(refs[:count], refs[count:2 * count]):
            total += matmul(c[...], w[...], ((1,), (1,)))
        refs[2 * count][...] = total.astype(BF16)

    by_row = lambda a: pl.BlockSpec((tile, a.shape[1]), lambda i, m: (i, 0))
    return pl.pallas_call(
        kernel,
        grid_spec=pltpu.PrefetchScalarGridSpec(
            num_scalar_prefetch=1,
            grid=(rows // tile,),
            in_specs=[by_row(up_wide), pl.BlockSpec(slot_down.shape, lambda i, m: (0, 0))]
            + [by_row(c) for c in cots]
            + [pl.BlockSpec((width, cols), lambda i, m, p=p: (0, m[0] ^ p)) for p in range(count)],
            out_specs=pl.BlockSpec((tile, width), lambda i, m: (i, 0)),
        ),
        out_shape=jax.ShapeDtypeStruct((rows, width), BF16),
        compiler_params=pltpu.CompilerParams(vmem_limit_bytes=48 * 1024 * 1024),
        cost_estimate=lasting(11.0),
        name="input_gradient",
    )(mp_at, up_wide, slot_down, *cots, *([weight] * count))


def make_shards(n_dp, n_mp):
    order = ring_order(n_dp)
    place = [order.index(e) for e in range(n_dp)]
    forward = [(order[i], order[(i + 1) % n_dp]) for i in range(n_dp)]
    backward = [(b, a) for a, b in forward]
    half_way = n_dp // 2

    def tables(stored):
        rows = []
        for e in range(n_dp):
            arrives, ring = [], []
            for owner in range(n_dp):
                ahead = (place[owner] - place[e]) % n_dp
                arrives += [n_dp - 1 if ahead == half_way else ahead - (ahead > half_way)] * stored
                ring += [ahead * stored + j for j in range(stored)]
            rows.append([arrives, ring])
        return rows

    def mp_pairs(bit):
        return [(i, i ^ bit) for i in range(n_mp)]

    def shards(
        tokens,
        value_weight,
        adapter_down_panels,
        adapter_up_panels,
        cotangent,
        block_list_entry,
        device_tenant_list,
        tenant_location_map,
    ):
        rows, width = tokens.shape
        stored, rank, _ = adapter_down_panels.shape
        out_width = adapter_up_panels.shape[2]
        blocks = block_list_entry.shape[0]
        block_rows = rows // blocks
        listed = device_tenant_list.shape[0]
        tenants = tenant_location_map.shape[0]
        half = width // 2

        dp_at = lax.axis_index("dp")
        mp_at = lax.axis_index("mp")
        mp_ref = mp_at.reshape(1)
        at_tables = jnp.asarray(tables(stored), jnp.int32)
        mine = lax.dynamic_index_in_dim(at_tables, dp_at, keepdims=False)
        arrives_at, ring_at = mine[0], mine[1]

        def mp_parts(value):
            bit = 1
            while True:
                got = lax.ppermute(value, "mp", mp_pairs(bit))
                bit *= 2
                if bit >= n_mp:
                    return value, got
                value = value + got

        up_all = lax.all_to_all(
            jnp.broadcast_to(adapter_up_panels[None], (n_dp,) + adapter_up_panels.shape),
            "dp", split_axis=0, concat_axis=0, tiled=True,
        ).reshape(tenants, rank, out_width)

        tenant_ids = jnp.arange(tenants, dtype=jnp.int32)
        list_location = jnp.sum(
            jnp.where(device_tenant_list[:, None] == tenant_ids[None, :], tenant_location_map[None, :], 0), axis=1
        )
        slot_ids = jnp.arange(listed, dtype=jnp.int32)
        row_slot = jnp.repeat(block_list_entry, block_rows)[:, None]
        at_list = lambda table: jnp.sum(
            jnp.where(list_location[:, None] == tenant_ids[None, :], table[None, :], 0), axis=1
        )

        where = at_list(arrives_at)
        which = at_list(jnp.asarray([j % stored for j in range(tenants)], jnp.int32))

        def both_ways(ahead, back):
            return [lax.ppermute(ahead, "dp", forward), lax.ppermute(back, "dp", backward)]

        def message(k, ahead, back):
            got_ahead, got_back = ahead.astype(F32), back.astype(F32)
            if ahead.shape[1] < width:
                got_ahead = jnp.pad(got_ahead, ((0, 0), (0, width - half)))
                got_back = jnp.pad(got_back, ((0, 0), (half, 0)))
            return [
                (dense[k].astype(F32) + got_ahead).astype(BF16),
                (dense[n_dp - k].astype(F32) + got_back).astype(BF16),
            ]

        held = [[adapter_down_panels, adapter_down_panels]]
        opposite, sums, cots = None, None, None
        last_in, last_out = half_way - 1, half_way + 1
        for phase in range(last_out + 1):
            now = {}
            if phase < last_in:
                now["held"] = both_ways(*held[-1])
            elif phase == last_in:
                now["opposite"] = both_ways(held[-1][0][:, :, :half], held[-1][1][:, :, half:])
            if phase == 2:
                now["sums"] = both_ways(*far_halves)
            elif phase > 2:
                now["sums"] = both_ways(*message(half_way + 2 - phase, *sums))
            if phase == 0:
                now["ups"] = [up_all]
                ready, *now["held"] = after([tokens] + now["held"])
                *products, others = base_products(mp_ref, ready, value_weight, n_mp)
                now["base"] = products + [others]
            elif phase == 1:
                up_part, own_ups = up_products(list_location, up_all, cotangent, row_slot, rank)
                far = (half_way * stored, half_way * stored + stored)
                now["shares"] = share_panels(
                    at_list(ring_at), mp_parts(up_part), row_slot, tokens, tenants, far
                )
                *products, others = base
                now["base"] = products + [lax.ppermute(others, "mp", mp_pairs(1))]
            elif phase == 2:
                *products, from_core = base
                base = [b + from_core[:, i * out_width:(i + 1) * out_width] for i, b in enumerate(products)]
                while len(base) > 1:
                    count = len(base) // 2
                    got = [lax.ppermute(b.astype(BF16), "mp", mp_pairs(2 * count)) for b in base[count:]]
                    base = [b + g.astype(F32) for b, g in zip(base, got)]
                now["base"] = base
            elif phase == 3:
                cots = [cotangent]
                bit = n_mp // 2
                while bit > 1:
                    cots += [lax.ppermute(c, "mp", mp_pairs(bit)) for c in cots]
                    bit //= 2
                now["cots"] = cots
            if phase == last_in + 1:
                slot_down = pick_panels(
                    [h[1] for h in held] + [h[0] for h in held[:0:-1]], opposite, where, which
                ).reshape(listed * rank, width)
                now["down"] = [slot_down] + list(mp_parts(down_products(tokens, slot_down, row_slot, rank)))

            keys = list(now)
            tied = after([v for k in keys for v in now[k]])
            for k in keys:
                now[k], tied = tied[:len(now[k])], tied[len(now[k]):]
            if "held" in now:
                held.append(now["held"])
            opposite, sums = now.get("opposite", opposite), now.get("sums", sums)
            base, cots = now.get("base", base if phase else None), now.get("cots", cots)
            if "ups" in now:
                (up_all,) = now["ups"]
            if "shares" in now:
                dense, up_wide, *far_halves = now["shares"]
                dense = dense.reshape(n_dp, stored * rank, width)
            if "down" in now:
                slot_down, *down_parts = now["down"]
        grad_a = add_panels(dense.reshape(-1, width), *sums).reshape(stored, rank, width)

        share_b, down_wide = share_panels(list_location, down_parts, row_slot, cotangent, tenants)
        values = (base[0] + matmul(down_wide, own_ups)).astype(BF16)

        all_cots = []
        for c in cots:
            all_cots += [c, lax.ppermute(c, "mp", mp_pairs(1))]
        token_gradient = input_gradient(mp_ref, all_cots, value_weight, up_wide, slot_down)

        back_b = lax.all_to_all(
            share_b.reshape(tenants, rank, out_width), "dp", split_axis=0, concat_axis=0, tiled=True
        ).reshape(n_dp, stored, rank, out_width)
        grad_b = jnp.sum(back_b.astype(F32), axis=0).astype(BF16)
        return (values, token_gradient, grad_a, grad_b)

    return shards


def solution(mesh):
    in_specs = (
        P("dp", "mp"),
        P("mp", None),
        P("dp", None, "mp"),
        P("dp", None, "mp"),
        P("dp", "mp"),
        P("dp"),
        P("dp"),
        P(),
    )
    out_specs = (P("dp", "mp"), P("dp", "mp"), P("dp", None, "mp"), P("dp", None, "mp"))
    shards = make_shards(mesh.shape["dp"], mesh.shape["mp"])
    return jax.shard_map(shards, mesh=mesh, in_specs=in_specs, out_specs=out_specs, check_vma=False)
```

```python
import jax
import jax.numpy as jnp
from jax import lax
from jax.experimental import pallas as pl
from jax.experimental.pallas import tpu as pltpu
from jax.sharding import PartitionSpec as P

F32 = jnp.float32
BF16 = jnp.bfloat16


def ring_order(n):
    cols = 1
    while 2 * (2 * cols) ** 2 <= n:
        cols *= 2
    rows = n // cols
    if cols < 2 or rows % 2 or rows * cols != n:
        return list(range(n))
    walk = [z * cols for z in range(rows)]
    for step, z in enumerate(reversed(range(rows))):
        across = range(1, cols) if step % 2 == 0 else reversed(range(1, cols))
        walk += [z * cols + x for x in across]
    return walk


def lasting(us):
    return pl.CostEstimate(flops=int(us * 0.05 * 1.1e9), bytes_accessed=int(us * 0.05 * 3.4e6), transcendentals=0)


def matmul(a, b, dims=((1,), (0,))):
    return lax.dot_general(a, b, (dims, ((), ())), preferred_element_type=F32)


def after(values):
    return list(lax.optimization_barrier(tuple(values)))


def pick_panels(sources, halves, where, which):
    slots = where.shape[0]
    _, rank, width = sources[0].shape
    n, cut = len(sources), width // 2

    def kernel(where_ref, which_ref, *refs):
        srcs, (left, right), dst, sem = refs[:n], refs[n:n + 2], refs[n + 2], refs[n + 3]

        @pl.loop(0, slots)
        def _(s):
            source, panel = where_ref[s], which_ref[s]
            for b in range(n):

                @pl.when(source == b)
                def _(b=b):
                    pltpu.make_async_copy(srcs[b].at[panel], dst.at[s], sem).start()

            @pl.when(source == n)
            def _():
                pltpu.make_async_copy(left.at[panel], dst.at[s, :, pl.ds(0, cut)], sem).start()
                pltpu.make_async_copy(right.at[panel], dst.at[s, :, pl.ds(cut, cut)], sem).start()

        pltpu.make_async_copy(dst, dst, sem).wait()

    smem = pl.BlockSpec(memory_space=pltpu.SMEM)
    return pl.pallas_call(
        kernel,
        in_specs=[smem, smem] + [pl.BlockSpec(memory_space=pl.ANY)] * (n + 2),
        out_specs=pl.BlockSpec(memory_space=pltpu.VMEM),
        out_shape=jax.ShapeDtypeStruct((slots, rank, width), BF16),
        scratch_shapes=[pltpu.SemaphoreType.DMA],
        compiler_params=pltpu.CompilerParams(vmem_limit_bytes=32 * 1024 * 1024),
        cost_estimate=lasting(2.5),
        name="pick_panels",
    )(where, which, *sources, *halves)


def by_slot(wide, slots, rank):
    low = jnp.zeros((wide.shape[0], rank), F32)
    for s in range(wide.shape[1] // rank):
        low += jnp.where(slots == s, wide[:, s * rank:(s + 1) * rank], 0.0)
    return low


def up_products(locations, up_all, cotangent, row_slot, rank):
    rows, out_width = cotangent.shape
    listed = locations.shape[0]

    def kernel(at_ref, up_ref, cot_ref, slot_ref, part_ref, own_ref):
        for s in range(listed):
            own_ref[s * rank:(s + 1) * rank, :] = up_ref[at_ref[s]]
        low = by_slot(matmul(cot_ref[...], own_ref[...], ((1,), (1,))), slot_ref[...], rank)
        part_ref[...] = jnp.concatenate([low[:rows // 2], low[rows // 2:]], axis=1)

    vmem = pl.BlockSpec(memory_space=pltpu.VMEM)
    return pl.pallas_call(
        kernel,
        in_specs=[pl.BlockSpec(memory_space=pltpu.SMEM), vmem, vmem, vmem],
        out_specs=[vmem, vmem],
        out_shape=[
            jax.ShapeDtypeStruct((rows // 2, 2 * rank), F32),
            jax.ShapeDtypeStruct((listed * rank, out_width), BF16),
        ],
        compiler_params=pltpu.CompilerParams(vmem_limit_bytes=48 * 1024 * 1024),
        cost_estimate=lasting(2.5),
        name="up_products",
    )(locations, up_all, cotangent, row_slot)


def down_products(tokens, slot_down, row_slot, rank):
    rows, width = tokens.shape
    tile = min(256, rows // 2)
    steps = rows // 2 // tile

    def kernel(first_ref, second_ref, down_ref, slot_a_ref, slot_b_ref, part_ref):
        halves = [
            by_slot(matmul(tok[...], down_ref[...], ((1,), (1,))), slot[...], rank)
            for tok, slot in ((first_ref, slot_a_ref), (second_ref, slot_b_ref))
        ]
        part_ref[...] = jnp.concatenate(halves, axis=1)

    upper, lower = lambda i: (i, 0), lambda i: (i + steps, 0)
    return pl.pallas_call(
        kernel,
        grid=(steps,),
        in_specs=[
            pl.BlockSpec((tile, width), upper),
            pl.BlockSpec((tile, width), lower),
            pl.BlockSpec(slot_down.shape, lambda i: (0, 0)),
            pl.BlockSpec((tile, 1), upper),
            pl.BlockSpec((tile, 1), lower),
        ],
        out_specs=pl.BlockSpec((tile, 2 * rank), upper),
        out_shape=jax.ShapeDtypeStruct((rows // 2, 2 * rank), F32),
        compiler_params=pltpu.CompilerParams(vmem_limit_bytes=48 * 1024 * 1024),
        cost_estimate=lasting(4.6),
        name="down_products",
    )(tokens, tokens, slot_down, row_slot, row_slot)


def share_panels(positions, parts, row_slot, lane_slot, other, panels, far=None):
    half_rows, pair = parts[0].shape
    rank, rows = pair // 2, 2 * half_rows
    listed, width = positions.shape[0], other.shape[1]
    tile = min(1024, width // 2 if far else width)
    steps = width // tile

    def kernel(at_ref, a_ref, b_ref, slot_ref, lane_ref, other_ref, dense_ref, wide_ref, *refs):
        turned_ref = refs[-1]
        step = pl.program_id(0)

        @pl.when(step == 0)
        def _():
            both = a_ref[...] + b_ref[...]
            low = jnp.concatenate([both[:, :rank], both[:, rank:]], axis=0).astype(BF16)
            column = lax.broadcasted_iota(jnp.int32, (rank, listed * rank), 1)
            eye = (column % rank == lax.broadcasted_iota(jnp.int32, (rank, listed * rank), 0)).astype(BF16)
            group = lax.broadcasted_iota(jnp.int32, (rows, listed * rank), 1) // rank
            wide = jnp.where(group == slot_ref[...], matmul(low, eye), 0.0)
            wide_ref[...] = wide.astype(BF16)
            turned = jnp.concatenate([both[:, :rank], both[:, rank:]], axis=0).T
            for s in range(listed):
                turned_ref[s * rank:(s + 1) * rank, :] = jnp.where(lane_ref[...] == s, turned, 0.0).astype(BF16)

        shares = matmul(turned_ref[...], other_ref[...]).astype(BF16)
        dense_ref[...] = jnp.zeros(dense_ref.shape, BF16)
        for s in range(listed):
            dense_ref[pl.ds(pl.multiple_of(at_ref[s] * rank, rank), rank), :] = shares[s * rank:(s + 1) * rank]
        if far:
            left_ref, right_ref = refs[:2]

            @pl.when(step < steps // 2)
            def _():
                left_ref[...] = dense_ref[far[0] * rank:far[1] * rank, :]

            @pl.when(step >= steps // 2)
            def _():
                right_ref[...] = dense_ref[far[0] * rank:far[1] * rank, :]

    whole = lambda a: pl.BlockSpec(a.shape, lambda i, at: (0, 0))
    out_specs = [
        pl.BlockSpec((panels * rank, tile), lambda i, at: (0, i)),
        pl.BlockSpec((rows, listed * rank), lambda i, at: (0, 0)),
    ]
    out_shape = [
        jax.ShapeDtypeStruct((panels * rank, width), BF16),
        jax.ShapeDtypeStruct((rows, listed * rank), BF16),
    ]
    if far:
        tall = (far[1] - far[0]) * rank
        out_specs += [
            pl.BlockSpec((tall, tile), lambda i, at: (0, jnp.minimum(i, steps // 2 - 1))),
            pl.BlockSpec((tall, tile), lambda i, at: (0, jnp.maximum(i - steps // 2, 0))),
        ]
        out_shape += [jax.ShapeDtypeStruct((tall, width // 2), BF16)] * 2
    return pl.pallas_call(
        kernel,
        grid_spec=pltpu.PrefetchScalarGridSpec(
            num_scalar_prefetch=1,
            grid=(steps,),
            in_specs=[whole(parts[0]), whole(parts[1]), whole(row_slot), whole(lane_slot), pl.BlockSpec((rows, tile), lambda i, at: (0, i))],
            out_specs=out_specs,
            scratch_shapes=[pltpu.VMEM((listed * rank, rows), BF16)],
        ),
        out_shape=out_shape,
        compiler_params=pltpu.CompilerParams(vmem_limit_bytes=48 * 1024 * 1024),
        cost_estimate=lasting(7.5),
        name="share_panels",
    )(positions, *parts, row_slot, lane_slot, other)


def add_panels(first, *others):
    rows, width = others[0].shape
    tile = min(512, width)

    def kernel(*refs):
        total = refs[0][...].astype(F32)
        for ref in refs[1:-1]:
            total += ref[...].astype(F32)
        refs[-1][...] = total.astype(BF16)

    spec = pl.BlockSpec((rows, tile), lambda i: (0, i))
    return pl.pallas_call(
        kernel,
        grid=(width // tile,),
        in_specs=[spec] * (1 + len(others)),
        out_specs=spec,
        out_shape=jax.ShapeDtypeStruct((rows, width), BF16),
        cost_estimate=lasting(260.0),
        name="add_panels",
    )(first, *others)


def base_products(mp_at, tokens, weight, count):
    rows, width = tokens.shape
    cols = weight.shape[1] // count
    tile = min(256, rows)

    def kernel(at_ref, tok_ref, *refs):
        weights, outs = refs[:count], refs[count:]
        for p in range(1, count, 2):
            outs[-1][:, p // 2 * cols:(p // 2 + 1) * cols] = matmul(tok_ref[...], weights[p][...])
        for p in range(0, count, 2):
            outs[p // 2][...] = matmul(tok_ref[...], weights[p][...])

    return pl.pallas_call(
        kernel,
        grid_spec=pltpu.PrefetchScalarGridSpec(
            num_scalar_prefetch=1,
            grid=(rows // tile,),
            in_specs=[pl.BlockSpec((tile, width), lambda i, m: (i, 0))]
            + [pl.BlockSpec((width, cols), lambda i, m, p=p: (0, m[0] ^ p)) for p in range(count)],
            out_specs=[pl.BlockSpec((tile, cols), lambda i, m: (i, 0))] * (count // 2)
            + [pl.BlockSpec((tile, count // 2 * cols), lambda i, m: (i, 0))],
        ),
        out_shape=[jax.ShapeDtypeStruct((rows, cols), F32)] * (count // 2)
        + [jax.ShapeDtypeStruct((rows, count // 2 * cols), F32)],
        compiler_params=pltpu.CompilerParams(vmem_limit_bytes=48 * 1024 * 1024),
        cost_estimate=lasting(170.0),
        name="base_products",
    )(mp_at, tokens, *([weight] * count))


def input_gradient(mp_at, cots, weight, up_wide, slot_down):
    rows = up_wide.shape[0]
    width = slot_down.shape[1]
    count = len(cots)
    cols = weight.shape[1] // count
    tile = min(256, rows)

    def kernel(at_ref, up_ref, slot_ref, *refs):
        total = matmul(up_ref[...], slot_ref[...])
        for c, w in zip(refs[:count], refs[count:2 * count]):
            total += matmul(c[...], w[...], ((1,), (1,)))
        refs[2 * count][...] = total.astype(BF16)

    by_row = lambda a: pl.BlockSpec((tile, a.shape[1]), lambda i, m: (i, 0))
    return pl.pallas_call(
        kernel,
        grid_spec=pltpu.PrefetchScalarGridSpec(
            num_scalar_prefetch=1,
            grid=(rows // tile,),
            in_specs=[by_row(up_wide), pl.BlockSpec(slot_down.shape, lambda i, m: (0, 0))]
            + [by_row(c) for c in cots]
            + [pl.BlockSpec((width, cols), lambda i, m, p=p: (0, m[0] ^ p)) for p in range(count)],
            out_specs=pl.BlockSpec((tile, width), lambda i, m: (i, 0)),
        ),
        out_shape=jax.ShapeDtypeStruct((rows, width), BF16),
        compiler_params=pltpu.CompilerParams(vmem_limit_bytes=48 * 1024 * 1024),
        cost_estimate=lasting(11.0),
        name="input_gradient",
    )(mp_at, up_wide, slot_down, *cots, *([weight] * count))


def make_shards(n_dp, n_mp):
    order = ring_order(n_dp)
    place = [order.index(e) for e in range(n_dp)]
    forward = [(order[i], order[(i + 1) % n_dp]) for i in range(n_dp)]
    backward = [(b, a) for a, b in forward]
    half_way = n_dp // 2

    def tables(stored):
        rows = []
        for e in range(n_dp):
            arrives, ring = [], []
            for owner in range(n_dp):
                ahead = (place[owner] - place[e]) % n_dp
                arrives += [n_dp - 1 if ahead == half_way else ahead - (ahead > half_way)] * stored
                ring += [ahead * stored + j for j in range(stored)]
            rows.append([arrives, ring])
        return rows

    def mp_pairs(bit):
        return [(i, i ^ bit) for i in range(n_mp)]

    def shards(
        tokens,
        value_weight,
        adapter_down_panels,
        adapter_up_panels,
        cotangent,
        block_list_entry,
        device_tenant_list,
        tenant_location_map,
    ):
        rows, width = tokens.shape
        stored, rank, _ = adapter_down_panels.shape
        out_width = adapter_up_panels.shape[2]
        blocks = block_list_entry.shape[0]
        block_rows = rows // blocks
        listed = device_tenant_list.shape[0]
        tenants = tenant_location_map.shape[0]
        half = width // 2

        dp_at = lax.axis_index("dp")
        mp_at = lax.axis_index("mp")
        mp_ref = mp_at.reshape(1)
        at_tables = jnp.asarray(tables(stored), jnp.int32)
        mine = lax.dynamic_index_in_dim(at_tables, dp_at, keepdims=False)
        arrives_at, ring_at = mine[0], mine[1]

        def mp_parts(value):
            bit = 1
            while True:
                got = lax.ppermute(value, "mp", mp_pairs(bit))
                bit *= 2
                if bit >= n_mp:
                    return value, got
                value = value + got

        up_all = lax.all_to_all(
            jnp.broadcast_to(adapter_up_panels[None], (n_dp,) + adapter_up_panels.shape),
            "dp", split_axis=0, concat_axis=0, tiled=True,
        ).reshape(tenants, rank, out_width)

        tenant_ids = jnp.arange(tenants, dtype=jnp.int32)
        list_location = jnp.sum(
            jnp.where(device_tenant_list[:, None] == tenant_ids[None, :], tenant_location_map[None, :], 0), axis=1
        )
        slot_ids = jnp.arange(listed, dtype=jnp.int32)
        row_slot = jnp.repeat(block_list_entry, block_rows)[:, None]
        lane_slot = row_slot.reshape(1, rows)
        at_list = lambda table: jnp.sum(
            jnp.where(list_location[:, None] == tenant_ids[None, :], table[None, :], 0), axis=1
        )

        where, share_place = at_list(arrives_at), at_list(ring_at)
        which = at_list(jnp.asarray([j % stored for j in range(tenants)], jnp.int32))

        def both_ways(ahead, back):
            return [lax.ppermute(ahead, "dp", forward), lax.ppermute(back, "dp", backward)]

        def message(k, ahead, back):
            got_ahead, got_back = ahead.astype(F32), back.astype(F32)
            if ahead.shape[1] < width:
                got_ahead = jnp.pad(got_ahead, ((0, 0), (0, width - half)))
                got_back = jnp.pad(got_back, ((0, 0), (half, 0)))
            return [
                (dense[k].astype(F32) + got_ahead).astype(BF16),
                (dense[n_dp - k].astype(F32) + got_back).astype(BF16),
            ]

        held = [[adapter_down_panels, adapter_down_panels]]
        opposite, sums, cots = None, None, None
        last_in, last_out = half_way - 1, half_way + 1
        for phase in range(last_out + 1):
            now = {}
            if phase < last_in:
                now["held"] = both_ways(*held[-1])
            elif phase == last_in:
                now["opposite"] = both_ways(held[-1][0][:, :, :half], held[-1][1][:, :, half:])
            if phase == 2:
                now["sums"] = both_ways(*far_halves)
            elif phase > 2:
                now["sums"] = both_ways(*message(half_way + 2 - phase, *sums))
            if phase == 0:
                now["ups"] = [up_all]
                now["index"] = [row_slot, lane_slot, list_location, share_place, where, which]
                ready, *now["held"] = after([tokens] + now["held"])
                *products, others = base_products(mp_ref, ready, value_weight, n_mp)
                now["base"] = products + [others]
            elif phase == 1:
                up_part, own_ups = up_products(list_location, up_all, cotangent, row_slot, rank)
                far = (half_way * stored, half_way * stored + stored)
                now["shares"] = share_panels(
                    share_place, mp_parts(up_part), row_slot, lane_slot, tokens, tenants, far
                )
                *products, others = base
                now["base"] = products + [lax.ppermute(others, "mp", mp_pairs(1))]
            elif phase == 2:
                *products, from_core = base
                base = [b + from_core[:, i * out_width:(i + 1) * out_width] for i, b in enumerate(products)]
                while len(base) > 1:
                    count = len(base) // 2
                    got = [lax.ppermute(b.astype(BF16), "mp", mp_pairs(2 * count)) for b in base[count:]]
                    base = [b + g.astype(F32) for b, g in zip(base, got)]
                now["base"] = base
            elif phase == 3:
                cots = [cotangent]
                bit = n_mp // 2
                while bit > 1:
                    cots += [lax.ppermute(c, "mp", mp_pairs(bit)) for c in cots]
                    bit //= 2
                now["cots"] = cots
            if phase == last_in + 1:
                slot_down = pick_panels(
                    [h[1] for h in held] + [h[0] for h in held[:0:-1]], opposite, where, which
                ).reshape(listed * rank, width)
                now["down"] = [slot_down] + list(mp_parts(down_products(tokens, slot_down, row_slot, rank)))

            keys = list(now)
            tied = after([v for k in keys for v in now[k]])
            for k in keys:
                now[k], tied = tied[:len(now[k])], tied[len(now[k]):]
            if "held" in now:
                held.append(now["held"])
            opposite, sums = now.get("opposite", opposite), now.get("sums", sums)
            base, cots = now.get("base", base if phase else None), now.get("cots", cots)
            if "ups" in now:
                (up_all,) = now["ups"]
                row_slot, lane_slot, list_location, share_place, where, which = now["index"]
            if "shares" in now:
                dense, up_wide, *far_halves = now["shares"]
                dense = dense.reshape(n_dp, stored * rank, width)
            if "down" in now:
                slot_down, *down_parts = now["down"]
        grad_a = add_panels(dense.reshape(-1, width), *sums).reshape(stored, rank, width)

        share_b, down_wide = share_panels(list_location, down_parts, row_slot, lane_slot, cotangent, tenants)
        values = (base[0] + matmul(down_wide, own_ups)).astype(BF16)

        all_cots = []
        for c in cots:
            all_cots += [c, lax.ppermute(c, "mp", mp_pairs(1))]
        token_gradient = input_gradient(mp_ref, all_cots, value_weight, up_wide, slot_down)

        back_b = lax.all_to_all(
            share_b.reshape(tenants, rank, out_width), "dp", split_axis=0, concat_axis=0, tiled=True
        ).reshape(n_dp, stored, rank, out_width)
        grad_b = jnp.sum(back_b.astype(F32), axis=0).astype(BF16)
        return (values, token_gradient, grad_a, grad_b)

    return shards


def solution(mesh):
    in_specs = (
        P("dp", "mp"),
        P("mp", None),
        P("dp", None, "mp"),
        P("dp", None, "mp"),
        P("dp", "mp"),
        P("dp"),
        P("dp"),
        P(),
    )
    out_specs = (P("dp", "mp"), P("dp", "mp"), P("dp", None, "mp"), P("dp", None, "mp"))
    shards = make_shards(mesh.shape["dp"], mesh.shape["mp"])
    return jax.shard_map(shards, mesh=mesh, in_specs=in_specs, out_specs=out_specs, check_vma=False)
```
